32 devices in a mesh: trip: 16 (over z, y, core), dens: 2 (over x).
Axes of the slice: x: 2, y: 2, z: 4, core: 2. Of those that a mesh axis runs over, the one named last changes fastest.
Arguments:
- amplitudes: bfloat16 [16, 8, 5625], P('trip', 'dens'), may hold values from -6 to 6
- integrals: bfloat16 [16, 8, 8, 75, 2850], P('trip', 'dens'), may hold values from -0.75 to 0.75
- pair_orbitals: int32 [16, 2], replicated, may hold values from 0 to 149
- pair_of_triple: int32 [128], P('trip'), may hold values from 0 to 15
- live_count: int32 [16], P('trip'), may hold values from 1 to 8, 48 in all
- k_orbital: int32 [16], P('trip'), may hold values from 0 to 149
- occ_irrep: int32 [150], replicated, may hold values from 0 to 7
- occ_energy: float32 [150], replicated, may hold values from -2 to -0.4
- vir_energy: float32 [8, 75], replicated, may hold values from 0.4 to 3
Outputs:
- lambda_two: float32 [16, 8, 5625], P('trip', 'dens')
- density: float32 [8, 5625], P('dens')
The draws below stay inside these ranges and needn't reach their ends.
Inputs may be any that keep to these rules, and one draw needn't show every extreme that they name: Block t works on its first live_count[t] triple positions; some block has all 8 live.
All inputs are finite; a program needn't handle non-finite values.
Results may differ from the reference program's by a relative error of at most 0.0003.
Values may be sent and summed in bfloat16 or wider, within the bound.
No kernel may reach another device: no remote copies, remote signals or barrier semaphores. Data moves between devices by JAX's collectives and lax.ppermute only.
A program may use at most 128 MiB of HBM per device.

```python
import math
import jax
import jax.numpy as jnp
import numpy as np
from jax import lax

NO = 150
NIRR = 8
VI = 75
CSLAB = 38
TPD = 8
PAIRS = 16
TRIPLES = 128
N_TRIP = 16


def plant(result, stream_key, smallest, high):
    spot = [jax.random.randint(jax.random.fold_in(stream_key, axis), (), 0, length) for axis, length in enumerate(result.shape)]
    longest = result.shape.index(max(result.shape))
    beside = spot[:longest] + [(spot[longest] + 1) % result.shape[longest]] + spot[longest + 1:]
    return result.at[tuple(spot)].set(smallest).at[tuple(beside)].set(high)


def block_scale(own_key, extent, split, low, largest):
    def one(dim, parts):
        draws = jax.random.uniform(jax.random.fold_in(jax.random.fold_in(own_key, 6), dim), (parts,), jnp.float32, low / len(split), largest / len(split))
        return jnp.repeat(jnp.exp(draws), extent[dim] // parts).reshape((-1,) + (1,) * (len(extent) - dim - 1))

    gain = one(*split[0])
    for cut in split[1:]:
        gain = gain * one(*cut)
    return gain


def profile(amount, total, most, lean):
    loads = [(1 << 20) // math.isqrt(standing ** lean) + 1 for standing in range(2, amount + 1)]
    surplus, holding = total - most - (amount - 1), [1] * (amount - 1)
    while surplus > 0:
        candidates = [i for i in range(amount - 1) if holding[i] < most]
        mass, budget = sum([loads[i] for i in candidates]), surplus
        for i in candidates:
            extra = min(most - holding[i], max(1, budget * loads[i] // mass), surplus)
            holding[i] = holding[i] + extra
            surplus = surplus - extra
    return np.array([most] + holding)


def uneven_parts(stream_key, number_of, total, reach, slope):
    if number_of == 2:
        one = jax.random.randint(stream_key, (), max(1, total - reach), min(reach, total - 1) + 1)
        return jnp.stack([one, total - one])
    tallies = jnp.asarray(profile(number_of, total, reach, slope), jnp.int32)
    couples = (number_of - 1) // 2
    source_of, taker = tallies[1:1 + 2 * couples:2], tallies[2:2 + 2 * couples:2]
    margin = jnp.minimum(source_of - 1, reach - taker)
    moved = jax.random.randint(jax.random.fold_in(stream_key, 1), (couples,), 0, 1 << 20) % (margin + 1)
    tallies = tallies.at[1:1 + 2 * couples:2].set(source_of - moved).at[2:2 + 2 * couples:2].set(taker + moved)
    return tallies[jax.random.permutation(jax.random.fold_in(stream_key, 2), number_of)]


def noise(stream_key, shape, scale, reach, pieces=(), held_as=jnp.bfloat16):
    values = scale * jax.random.normal(stream_key, shape, jnp.float32)
    if pieces:
        values = values * block_scale(stream_key, shape, pieces, -0.22, 0.18)
    return jnp.clip(values, -reach, reach).astype(held_as)


def setup_inputs(seed: int = 0) -> dict:
    seeds = jax.random.split(jax.random.key(seed), 10)
    amplitudes = noise(seeds[0], (PAIRS, NIRR, VI * VI), 1.0, 6.0, ((0, 16), (1, 2)))
    integrals = noise(seeds[1], (N_TRIP, NIRR, NIRR, VI, VI * CSLAB), VI ** -0.5, 0.75, ((0, 16), (1, 2)))
    pair_orbitals = plant(jax.random.randint(seeds[2], (PAIRS, 2), 0, NO), jax.random.fold_in(seeds[2], 1), 0, NO - 1).astype(jnp.int32)
    pair_of_triple = plant(jax.random.randint(seeds[3], (TRIPLES,), 0, PAIRS), jax.random.fold_in(seeds[3], 1), 0, PAIRS - 1).astype(jnp.int32)
    live_count = uneven_parts(seeds[4], N_TRIP, 3 * N_TRIP, TPD, 1).astype(jnp.int32)
    k_orbital = plant(jax.random.randint(seeds[5], (N_TRIP,), 0, NO), jax.random.fold_in(seeds[5], 1), 0, NO - 1).astype(jnp.int32)
    occ_irrep = plant(jax.random.randint(seeds[6], (NO,), 0, NIRR), jax.random.fold_in(seeds[6], 1), 0, NIRR - 1).astype(jnp.int32)
    occ_energy = jnp.clip(jax.random.uniform(seeds[7], (NO,), jnp.float32, -2.0, -0.4), -2.0, -0.4)
    vir_energy = jnp.clip(jax.random.uniform(seeds[8], (NIRR, VI), jnp.float32, 0.4, 3.0), 0.4, 3.0)
    return dict(amplitudes=amplitudes, integrals=integrals, pair_orbitals=pair_orbitals, pair_of_triple=pair_of_triple, live_count=live_count, k_orbital=k_orbital, occ_irrep=occ_irrep, occ_energy=occ_energy, vir_energy=vir_energy)


def rounded(value):
    return lax.optimization_barrier(value.astype(jnp.bfloat16)).astype(jnp.float32)


def reference(amplitudes, integrals, pair_orbitals, pair_of_triple, live_count, k_orbital, occ_irrep, occ_energy, vir_energy):
    tile_blocks = amplitudes.reshape(PAIRS, NIRR, VI, VI)
    irrep_ids = jnp.arange(NIRR, dtype=jnp.int32)
    pair_table = pair_of_triple.reshape(N_TRIP, TPD)

    def one_triple(integral_k, k_irrep, k_energy, pair_id, running):
        lambda_acc, density_acc = running
        orb_i = pair_orbitals[pair_id, 0]
        orb_j = pair_orbitals[pair_id, 1]
        ij_irrep = jnp.bitwise_xor(occ_irrep[orb_i], occ_irrep[orb_j])
        ijk_energy = occ_energy[orb_i] + occ_energy[orb_j] + k_energy
        tile = tile_blocks[pair_id].astype(jnp.float32)
        col_block = jnp.take(tile, jnp.bitwise_xor(irrep_ids, ij_irrep), axis=0)
        lambda_sum = jnp.zeros((NIRR, VI, VI), jnp.float32)
        density_sum = jnp.zeros((NIRR, VI, VI), jnp.float32)
        for c_irrep in range(NIRR):
            b_irrep = jnp.bitwise_xor(jnp.bitwise_xor(irrep_ids, jnp.bitwise_xor(ij_irrep, k_irrep)), c_irrep)
            g_blocks = jnp.take(integral_k[c_irrep], b_irrep, axis=0).astype(jnp.float32)
            energy_b = jnp.take(vir_energy, b_irrep, axis=0)
            energy_c = vir_energy[c_irrep, :CSLAB]
            denominator = ijk_energy - vir_energy[:, :, None] - (energy_b[:, :, None] + energy_c[None, None, :]).reshape(NIRR, 1, VI * CSLAB)
            weights = jnp.einsum('gad,gdx->gax', tile, g_blocks)
            scaled = rounded(weights / denominator)
            swapped = rounded(jnp.einsum('gde,gdx->gex', col_block, g_blocks))
            lambda_sum = lambda_sum + jnp.einsum('gax,gdx->gad', scaled, g_blocks)
            density_sum = density_sum + jnp.einsum('gax,gex->gae', scaled, swapped)
        lambda_acc = lambda_acc.at[pair_id].add(lambda_sum)
        return lambda_acc, density_acc + density_sum

    def per_device(running, inputs):
        integral_k, k_index, live_total, pair_ids = inputs
        k_irrep = occ_irrep[k_index]
        k_energy = occ_energy[k_index]

        def advance(position, state):
            return one_triple(integral_k, k_irrep, k_energy, pair_ids[position], state)

        return lax.fori_loop(0, live_total, advance, running), None

    initial = (jnp.zeros((PAIRS, NIRR, VI, VI), jnp.float32), jnp.zeros((NIRR, VI, VI), jnp.float32))
    (lambda_acc, density_acc), unused = lax.scan(per_device, initial, (integrals, k_orbital, live_count, pair_table))
    return lambda_acc.reshape(PAIRS, NIRR, VI * VI), (density_acc / TRIPLES).reshape(NIRR, VI * VI)
```

```python
import jax
import jax.numpy as jnp
from jax import lax
from jax.experimental import pallas as pl
from jax.experimental.pallas import tpu as pltpu
from jax.sharding import PartitionSpec as P

LANES = 128
MAIN = 64


def round_up(value, step):
    return -(-value // step) * step


def block_rows(width):
    return round_up(width, 16)


def packed_rows(width):
    return block_rows(width) // 2 + 8


def pack_blocks(blocks):
    width = blocks.shape[-1]
    rows, rest = block_rows(width), width - MAIN
    lead = blocks.shape[:-2]
    pad = [(0, 0)] * len(lead)
    blocks = jnp.pad(blocks, pad + [(0, rows - width), (0, 0)])
    main = jnp.concatenate([blocks[..., : rows // 2, :MAIN], blocks[..., rows // 2 :, :MAIN]], axis=-1)
    tail = blocks[..., MAIN:].reshape(lead + (rows // 8, 8, rest))
    tail = jnp.swapaxes(tail, -3, -2).reshape(lead + (8, rows // 8 * rest))
    tail = jnp.pad(tail, pad + [(0, 0), (0, LANES - rows // 8 * rest)])
    return jnp.concatenate([main, tail], axis=-2)


def unpack_blocks(packed, width):
    rows, rest = block_rows(width), width - MAIN
    lead = packed.shape[:-2]
    main = jnp.concatenate([packed[..., : rows // 2, :MAIN], packed[..., : rows // 2, MAIN:]], axis=-2)
    tail = packed[..., rows // 2 :, : rows // 8 * rest].reshape(lead + (8, rows // 8, rest))
    tail = jnp.swapaxes(tail, -3, -2).reshape(lead + (rows, rest))
    return jnp.concatenate([main, tail], axis=-1)[..., :width, :]


def partner(value, axis, bit):
    count = lax.axis_size(axis)
    return lax.ppermute(value, axis, [(i, i ^ bit) for i in range(count)])


def far_bits(axis):
    bits, bit = [], 2
    while bit < lax.axis_size(axis):
        bits.append(bit)
        bit *= 2
    return bits


def all_bits(axis):
    return [1] + far_bits(axis) if lax.axis_size(axis) > 1 else []


def reversed_bits(value, count):
    out = jnp.int32(0)
    for b in range(count):
        out = out | (((value >> b) & 1) << (count - 1 - b))
    return out


def term_kernel(
    dims,
    place_ref,
    meta_ref,
    pairs_ref,
    irrep_ref,
    energy_ref,
    amp_ref,
    vir_ref,
    y_ref,
    own_ref,
    recv_ref,
    out_ref,
    list_ref,
    size_ref,
    tile32,
    tile16,
    xcol,
    lam,
    gbuf,
    sems,
):
    width, per_dev, irr_local, dens, trip_bits, chunks, first = dims
    rows = block_rows(width)
    half, rest, groups = rows // 2, width - MAIN, rows // 8
    share = irr_local // 2
    low_mask = irr_local - 1
    steps = chunks * 2 * dens
    step = pl.program_id(0)
    my_trip, my_dens = place_ref[0], place_ref[1]

    def position(at):
        chunk = at // (2 * dens)
        within = at % (2 * dens)
        who, high = within // dens, within % dens
        k_irrep = irrep_ref[meta_ref[who, per_dev + 1]]
        h = high * irr_local + ((first + chunk) ^ (k_irrep & low_mask))
        return chunk, who, h, k_irrep

    def fetch(at, act):
        chunk, who, h, _ = position(at)
        slot = at % 2
        for part in range(share):
            for side, ref in enumerate((own_ref, recv_ref)):
                b_irrep = h ^ (my_dens * irr_local + side * share + part)

                @pl.when(who == side)
                def _():
                    copy = pltpu.make_async_copy(
                        ref.at[0, part, b_irrep], gbuf.at[slot, part], sems.at[slot, part]
                    )
                    act(copy)

    @pl.when(step == 0)
    def _():
        fetch(step, lambda copy: copy.start())
        out_ref[...] = jnp.zeros_like(out_ref)
        for who in range(2):
            size = jnp.int32(0)
            for s in range(per_dev):
                pair = meta_ref[who, s]
                fresh = s < meta_ref[who, per_dev]
                for earlier in range(s):
                    fresh = jnp.logical_and(fresh, meta_ref[who, earlier] != pair)

                @pl.when(fresh)
                def _():
                    list_ref[who, size] = pair

                size = size + fresh.astype(jnp.int32)
            size_ref[who] = size

    @pl.when(step + 1 < steps)
    def _():
        fetch(step + 1, lambda copy: copy.start())

    chunk, who, h, k_irrep = position(step)
    size = size_ref[who]
    k_energy = energy_ref[meta_ref[who, per_dev + 1]]
    lane = lax.broadcasted_iota(jnp.int32, (8, LANES), 1)

    def of_slot(j):
        pair = list_ref[who, j]
        orb_i, orb_j = pairs_ref[2 * pair], pairs_ref[2 * pair + 1]
        a_irrep = h ^ k_irrep ^ irrep_ref[orb_i] ^ irrep_ref[orb_j]
        gap = pair ^ my_trip
        spot = ((gap & 1) * dens + ((a_irrep // irr_local) ^ my_dens)) * (1 << trip_bits) + reversed_bits(
            gap >> 1, trip_bits
        )
        return pair, orb_i, orb_j, a_irrep, spot

    for j in range(per_dev):

        @pl.when(j < size)
        def _():
            pair, orb_i, orb_j, a_irrep, spot = of_slot(j)
            packed = amp_ref[spot * irr_local + (a_irrep & low_mask)].astype(jnp.float32)
            main, tail = packed[:half], packed[half:]
            turned = pltpu.roll(main, LANES - MAIN, 1)
            for q in range(groups):
                left = main[8 * q : 8 * q + 8] if 8 * q < half else turned[8 * q - half : 8 * q - half + 8]
                right = pltpu.roll(tail, (MAIN - rest * q) % LANES, 1)
                tile32[width * j + 8 * q : width * j + 8 * q + 8, :] = jnp.where(lane < MAIN, left, right)
            ijk_energy = energy_ref[orb_i] + energy_ref[orb_j] + k_energy
            xcol[width * j : width * j + rows, :] = ijk_energy - vir_ref[a_irrep]

    tile16[...] = tile32[:, :width].astype(jnp.bfloat16)
    fetch(step, lambda copy: copy.wait())
    slot = step % 2

    for live in range(1, per_dev + 1):
        used = round_up(width * live, 16)

        @pl.when(size == live)
        def _():
            def one(part, carry):
                b_irrep = h ^ (my_dens * irr_local + who * share + part)
                y_row = b_irrep * irr_local + who * share + part
                left = tile16[:used, :]
                x = xcol[:used, :]
                acc = jnp.zeros((used, width), jnp.float32)
                total = gbuf.shape[3]
                for start in range(0, total, 256):
                    stop = min(start + 256, total)
                    g = gbuf[slot, part, :, start:stop]
                    w = jnp.dot(left, g, preferred_element_type=jnp.float32)
                    y = y_ref[y_row][:, start:stop]
                    z = (w / (x - y)).astype(jnp.bfloat16)
                    acc = acc + lax.dot_general(
                        z, g, (((1,), (1,)), ((), ())), preferred_element_type=jnp.float32
                    )

                @pl.when(part == 0)
                def _():
                    lam[:used, :width] = acc

                @pl.when(part > 0)
                def _():
                    lam[:used, :width] = lam[:used, :width] + acc

                return carry

            lax.fori_loop(0, share, one, 0)

    for j in range(per_dev):

        @pl.when(j < size)
        def _():
            pair, _, _, _, spot = of_slot(j)
            copies = jnp.int32(0)
            for s in range(per_dev):
                same = jnp.logical_and(meta_ref[who, s] == pair, s < meta_ref[who, per_dev])
                copies = copies + same.astype(jnp.int32)
            weight = copies.astype(jnp.float32)
            place = spot * chunks + chunk
            tail = jnp.zeros((8, LANES), jnp.float32)
            for q in range(groups):
                block = lam[width * j + 8 * q : width * j + 8 * q + 8, :]
                moved = pltpu.roll(block, (rest * q - MAIN) % LANES, 1)
                here = jnp.logical_and(lane >= rest * q, lane < rest * q + rest)
                tail = jnp.where(here, moved, tail)
            top = lam[width * j : width * j + half, :]
            low = pltpu.roll(lam[width * j + half : width * j + rows, :], MAIN, 1)
            wide = lax.broadcasted_iota(jnp.int32, (half, LANES), 1)
            main = jnp.where(wide < MAIN, top, low)
            out_ref[place, :half, :] = out_ref[place, :half, :] + weight * main
            out_ref[place, half:, :] = out_ref[place, half:, :] + weight * tail


def pair_terms(dims, place, meta, pairs, irreps, energies, amps, vir_col, y_table, own, recv):
    width, per_dev, irr_local, dens, trip_bits, chunks, first = dims
    share = irr_local // 2
    tall = round_up(width * per_dev + block_rows(width) - width, 16)
    spots = 2 * dens * (1 << trip_bits)
    smem = pl.BlockSpec(memory_space=pltpu.SMEM)
    vmem = pl.BlockSpec(memory_space=pltpu.VMEM)
    hbm = pl.BlockSpec(memory_space=pl.ANY)
    return pl.pallas_call(
        lambda *refs: term_kernel(dims, *refs),
        grid=(chunks * 2 * dens,),
        in_specs=[smem] * 5 + [vmem] * 3 + [hbm] * 2,
        out_specs=vmem,
        out_shape=jax.ShapeDtypeStruct((spots * chunks, packed_rows(width), LANES), jnp.float32),
        scratch_shapes=[
            pltpu.SMEM((2, per_dev), jnp.int32),
            pltpu.SMEM((2,), jnp.int32),
            pltpu.VMEM((tall, LANES), jnp.float32),
            pltpu.VMEM((tall, width), jnp.bfloat16),
            pltpu.VMEM((tall, 1), jnp.float32),
            pltpu.VMEM((tall, LANES), jnp.float32),
            pltpu.VMEM((2, share) + own.shape[3:], jnp.bfloat16),
            pltpu.SemaphoreType.DMA((2, share)),
        ],
        compiler_params=pltpu.CompilerParams(vmem_limit_bytes=48 * 2**20),
        cost_estimate=pl.CostEstimate(flops=10**10, bytes_accessed=10**7, transcendentals=0),
        name="pair_terms",
    )(place, meta, pairs, irreps, energies, amps, vir_col, y_table, own, recv)


def body(
    amplitudes,
    integrals,
    pair_orbitals,
    pair_of_triple,
    live_count,
    k_orbital,
    occ_irrep,
    occ_energy,
    vir_energy,
):
    irr_local = amplitudes.shape[1]
    irreps, width = vir_energy.shape
    slab = integrals.shape[4] // width
    per_dev = pair_of_triple.shape[0]
    trip, dens = lax.axis_size("trip"), lax.axis_size("dens")
    trip_bits = len(far_bits("trip"))
    triple_total = per_dev * trip
    share = irr_local // 2
    my_trip, my_dens = lax.axis_index("trip"), lax.axis_index("dens")

    recv = partner(integrals[:, share:], "trip", 1)
    own_meta = jnp.concatenate([pair_of_triple, live_count, k_orbital])
    meta = jnp.stack([own_meta, partner(own_meta, "trip", 1)])
    place = jnp.stack([my_trip, my_dens]).astype(jnp.int32)

    amps = pack_blocks(amplitudes.reshape(irr_local, width, width))[None]
    for bit in reversed(far_bits("trip")):
        amps = jnp.concatenate([amps, partner(amps, "trip", bit)])
    for bit in all_bits("dens"):
        amps = jnp.concatenate([amps, partner(amps, "dens", bit)])
    amps = jnp.concatenate([amps, partner(amps, "trip", 1)])
    amps = amps.reshape((-1,) + amps.shape[2:])

    vir_col = jnp.pad(vir_energy, ((0, 0), (0, block_rows(width) - width)))[:, :, None]
    vir_mine = lax.dynamic_slice_in_dim(vir_energy, my_dens * irr_local, irr_local, 0)[:, :slab]
    y_table = jnp.repeat(vir_energy, slab, axis=1)[:, None, :] + jnp.tile(vir_mine, (1, width))[None, :, :]
    y_table = y_table.reshape(irreps * irr_local, 1, width * slab)

    dims = (width, per_dev, irr_local, dens, trip_bits, irr_local, 0)
    terms = pair_terms(
        dims, place, meta, pair_orbitals.reshape(-1), occ_irrep, occ_energy, amps, vir_col, y_table, integrals, recv
    )
    def halve(terms, axis, bit):
        count = terms.shape[0] // 2
        return terms[:count] + partner(terms[count:], axis, bit)

    terms = halve(terms, "trip", 1)
    for bit in reversed(all_bits("dens")):
        terms = halve(terms, "dens", bit)
    for bit in far_bits("trip"):
        terms = halve(terms, "trip", bit)

    orbitals = lax.dynamic_index_in_dim(pair_orbitals, my_trip, 0, keepdims=False)
    ij_irrep = jnp.bitwise_xor(occ_irrep[orbitals[0]], occ_irrep[orbitals[1]])
    local = jnp.arange(irr_local, dtype=jnp.int32)
    order = jnp.bitwise_xor(local, ij_irrep % irr_local)
    mine = jnp.take(unpack_blocks(terms, width), order, axis=0)
    amps_own = amps.reshape((2, dens, 1 << trip_bits, irr_local) + amps.shape[1:])[0, :, 0]
    amps_own = lax.dynamic_index_in_dim(amps_own, ij_irrep // irr_local, 0, keepdims=False)
    amps_own = jnp.take(unpack_blocks(amps_own, width), order, axis=0).astype(jnp.float32)
    density = jnp.einsum(
        "gad,gde->gae", mine, amps_own, precision=lax.Precision.HIGHEST, preferred_element_type=jnp.float32
    )
    density = density.reshape(irr_local, width * width)
    for bit in all_bits("trip"):
        density = density + partner(density, "trip", bit)
    return (mine.reshape(1, irr_local, width * width), density / triple_total)


def solution(mesh):
    in_specs = (
        P("trip", "dens", None),
        P("trip", "dens", None, None, None),
        P(),
        P("trip"),
        P("trip"),
        P("trip"),
        P(),
        P(),
        P(),
    )
    out_specs = (P("trip", "dens", None), P("dens", None))
    return jax.shard_map(body, mesh=mesh, in_specs=in_specs, out_specs=out_specs, check_vma=False)
```

```python
import jax
import jax.numpy as jnp
from jax import lax
from jax.experimental import pallas as pl
from jax.experimental.pallas import tpu as pltpu
from jax.sharding import PartitionSpec as P

LANES = 128
MAIN = 64


def round_up(value, step):
    return -(-value // step) * step


def block_rows(width):
    return round_up(width, 16)


def packed_rows(width):
    return block_rows(width) // 2 + 8


def pack_blocks(blocks):
    width = blocks.shape[-1]
    rows, rest = block_rows(width), width - MAIN
    lead = blocks.shape[:-2]
    pad = [(0, 0)] * len(lead)
    blocks = jnp.pad(blocks, pad + [(0, rows - width), (0, 0)])
    main = jnp.concatenate([blocks[..., : rows // 2, :MAIN], blocks[..., rows // 2 :, :MAIN]], axis=-1)
    tail = blocks[..., MAIN:].reshape(lead + (rows // 8, 8, rest))
    tail = jnp.swapaxes(tail, -3, -2).reshape(lead + (8, rows // 8 * rest))
    tail = jnp.pad(tail, pad + [(0, 0), (0, LANES - rows // 8 * rest)])
    return jnp.concatenate([main, tail], axis=-2)


def unpack_blocks(packed, width):
    rows, rest = block_rows(width), width - MAIN
    lead = packed.shape[:-2]
    main = jnp.concatenate([packed[..., : rows // 2, :MAIN], packed[..., : rows // 2, MAIN:]], axis=-2)
    tail = packed[..., rows // 2 :, : rows // 8 * rest].reshape(lead + (8, rows // 8, rest))
    tail = jnp.swapaxes(tail, -3, -2).reshape(lead + (rows, rest))
    return jnp.concatenate([main, tail], axis=-1)[..., :width, :]


def partner(value, axis, bit):
    count = lax.axis_size(axis)
    return lax.ppermute(value, axis, [(i, i ^ bit) for i in range(count)])


def far_bits(axis):
    bits, bit = [], 2
    while bit < lax.axis_size(axis):
        bits.append(bit)
        bit *= 2
    return bits


def all_bits(axis):
    return [1] + far_bits(axis) if lax.axis_size(axis) > 1 else []


def reversed_bits(value, count):
    out = jnp.int32(0)
    for b in range(count):
        out = out | (((value >> b) & 1) << (count - 1 - b))
    return out


def plan_kernel(
    per_dev, dens, trip_bits, place_ref, meta_ref, pairs_ref, irrep_ref, energy_ref, plan_ref, ijk_ref, list_ref
):
    for who in range(2):
        k_orbital = meta_ref[who, per_dev + 1]
        live = meta_ref[who, per_dev]
        size = jnp.int32(0)
        for s in range(per_dev):
            pair = meta_ref[who, s]
            fresh = s < live
            for earlier in range(s):
                fresh = jnp.logical_and(fresh, meta_ref[who, earlier] != pair)

            @pl.when(fresh)
            def _():
                list_ref[size] = pair

            size = size + fresh.astype(jnp.int32)
        plan_ref[who] = size
        plan_ref[2 + who] = irrep_ref[k_orbital]
        for j in range(per_dev):
            at = 4 + 4 * (who * per_dev + j)

            @pl.when(j < size)
            def _():
                pair = list_ref[j]
                orb_i, orb_j = pairs_ref[2 * pair], pairs_ref[2 * pair + 1]
                gap = pair ^ place_ref[0]
                copies = jnp.int32(0)
                for s in range(per_dev):
                    same = jnp.logical_and(meta_ref[who, s] == pair, s < live)
                    copies = copies + same.astype(jnp.int32)
                plan_ref[at] = irrep_ref[orb_i] ^ irrep_ref[orb_j] ^ irrep_ref[k_orbital]
                plan_ref[at + 1] = (gap & 1) * dens
                plan_ref[at + 2] = reversed_bits(gap >> 1, trip_bits)
                plan_ref[at + 3] = copies
                ijk_ref[who * per_dev + j] = energy_ref[orb_i] + energy_ref[orb_j] + energy_ref[k_orbital]


def make_plan(per_dev, dens, trip_bits, place, meta, pairs, irreps, energies):
    smem = pl.BlockSpec(memory_space=pltpu.SMEM)
    return pl.pallas_call(
        lambda *refs: plan_kernel(per_dev, dens, trip_bits, *refs),
        in_specs=[smem] * 5,
        out_specs=[smem] * 2,
        out_shape=[
            jax.ShapeDtypeStruct((4 + 8 * per_dev,), jnp.int32),
            jax.ShapeDtypeStruct((2 * per_dev,), jnp.float32),
        ],
        scratch_shapes=[pltpu.SMEM((per_dev,), jnp.int32)],
        name="plan",
    )(place, meta, pairs, irreps, energies)


def term_kernel(
    dims,
    place_ref,
    plan_ref,
    ijk_ref,
    amp_ref,
    vir_ref,
    y_ref,
    *refs,
):
    width, per_dev, irr_local, dens, trip_bits, sides, chunk = dims
    block_refs = refs[:sides]
    out_ref, tile32, tile16, xcol, lam, gbuf, sems = refs[sides:]
    rows = block_rows(width)
    half, rest, groups = rows // 2, width - MAIN, rows // 8
    share, irreps = irr_local // sides, irr_local * dens
    low_mask = irr_local - 1
    steps = sides * dens
    step = pl.program_id(0)
    my_dens = place_ref[1]

    def position(at):
        who, high = at // dens, at % dens
        return who, high * irr_local + (chunk ^ (plan_ref[2 + who] & low_mask))

    def fetch(at, act):
        who, h = position(at)
        slot = at % 2
        for part in range(share):
            for side, ref in enumerate(block_refs):
                b_irrep = h ^ (my_dens * irr_local + side * share + part)

                @pl.when(who == side)
                def _():
                    copy = pltpu.make_async_copy(
                        ref.at[0, part, b_irrep], gbuf.at[slot, part], sems.at[slot, part]
                    )
                    act(copy)

    @pl.when(step == 0)
    def _():
        fetch(step, lambda copy: copy.start())
        out_ref[...] = jnp.zeros_like(out_ref)

    @pl.when(step + 1 < steps)
    def _():
        fetch(step + 1, lambda copy: copy.start())

    who, h = position(step)
    slot = step % 2
    size = plan_ref[who]
    lane = lax.broadcasted_iota(jnp.int32, (8, LANES), 1)
    wide = lax.broadcasted_iota(jnp.int32, (half, LANES), 1)

    def of_slot(j):
        at = 4 + 4 * (who * per_dev + j)
        a_irrep = h ^ plan_ref[at]
        spot = (plan_ref[at + 1] + ((a_irrep // irr_local) ^ my_dens)) * (1 << trip_bits) + plan_ref[at + 2]
        return a_irrep, spot, plan_ref[at + 3]

    for live in range(1, per_dev + 1):
        used = round_up(width * live, 16)

        @pl.when(size == live)
        def _():
            for j in range(live):
                a_irrep, spot, _ = of_slot(j)
                packed = amp_ref[spot * irr_local + (a_irrep & low_mask)].astype(jnp.float32)
                main, tail = packed[:half], packed[half:]
                turned = pltpu.roll(main, LANES - MAIN, 1)
                for q in range(groups):
                    left = main[8 * q : 8 * q + 8] if 8 * q < half else turned[8 * q - half : 8 * q - half + 8]
                    right = pltpu.roll(tail, (MAIN - rest * q) % LANES, 1)
                    tile32[width * j + 8 * q : width * j + 8 * q + 8, :] = jnp.where(lane < MAIN, left, right)
                xcol[width * j : width * j + rows, :] = ijk_ref[who * per_dev + j] - vir_ref[a_irrep]
            tile16[:used, :] = tile32[:used, :width].astype(jnp.bfloat16)
            fetch(step, lambda copy: copy.wait())

            def one(part, carry):
                c_local = who * share + part
                y_row = (h ^ (my_dens * irr_local + c_local)) * irr_local + c_local
                left = tile16[:used, :]
                acc = jnp.zeros((used, width), jnp.float32)
                total = gbuf.shape[3]
                for start in range(0, total, 256):
                    stop = min(start + 256, total)
                    g = gbuf[slot, part, :, start:stop]
                    w = jnp.dot(left, g, preferred_element_type=jnp.float32)
                    x = xcol[:used, :]
                    x = jnp.concatenate([x, x], axis=1)[:, : stop - start]
                    z = (w / (x - y_ref[y_row][:, start:stop])).astype(jnp.bfloat16)
                    acc = acc + lax.dot_general(
                        z, g, (((1,), (1,)), ((), ())), preferred_element_type=jnp.float32
                    )

                @pl.when(part == 0)
                def _():
                    lam[:used, :width] = acc

                @pl.when(part > 0)
                def _():
                    lam[:used, :width] = lam[:used, :width] + acc

                return carry

            lax.fori_loop(0, share, one, 0)

            for j in range(live):
                _, spot, copies = of_slot(j)
                weight = copies.astype(jnp.float32)
                tail = jnp.zeros((8, LANES), jnp.float32)
                for q in range(groups):
                    block = lam[width * j + 8 * q : width * j + 8 * q + 8, :]
                    moved = pltpu.roll(block, (rest * q - MAIN) % LANES, 1)
                    here = jnp.logical_and(lane >= rest * q, lane < rest * q + rest)
                    tail = jnp.where(here, moved, tail)
                top = lam[width * j : width * j + half, :]
                low = pltpu.roll(lam[width * j + half : width * j + rows, :], MAIN, 1)
                main = jnp.where(wide < MAIN, top, low)
                out_ref[spot, :half, :] = out_ref[spot, :half, :] + weight * main
                out_ref[spot, half:, :] = out_ref[spot, half:, :] + weight * tail


def pair_terms(dims, place, plan, ijk, amps, vir_col, y_table, blocks):
    width, per_dev, irr_local, dens, trip_bits, sides, _ = dims
    share = irr_local // sides
    tall = round_up(width * per_dev + block_rows(width) - width, 16)
    spots = 2 * dens * (1 << trip_bits)
    smem = pl.BlockSpec(memory_space=pltpu.SMEM)
    vmem = pl.BlockSpec(memory_space=pltpu.VMEM)
    hbm = pl.BlockSpec(memory_space=pltpu.HBM)
    return pl.pallas_call(
        lambda *refs: term_kernel(dims, *refs),
        grid=(sides * dens,),
        in_specs=[smem] * 3 + [vmem] * 3 + [hbm] * sides,
        out_specs=vmem,
        out_shape=jax.ShapeDtypeStruct((spots, packed_rows(width), LANES), jnp.float32),
        scratch_shapes=[
            pltpu.VMEM((tall, LANES), jnp.float32),
            pltpu.VMEM((tall, width), jnp.bfloat16),
            pltpu.VMEM((tall, LANES), jnp.float32),
            pltpu.VMEM((tall, LANES), jnp.float32),
            pltpu.VMEM((2, share) + blocks[0].shape[3:], jnp.bfloat16),
            pltpu.SemaphoreType.DMA((2, share)),
        ],
        compiler_params=pltpu.CompilerParams(vmem_limit_bytes=48 * 2**20),
        cost_estimate=pl.CostEstimate(flops=14 * 10**9, bytes_accessed=10**7, transcendentals=0),
        name="pair_terms",
    )(place, plan, ijk, amps, vir_col, y_table, *blocks)


def settle(blocks):
    hbm = pl.BlockSpec(memory_space=pltpu.HBM)
    return pl.pallas_call(
        lambda source, target: None,
        in_specs=[hbm],
        out_specs=hbm,
        out_shape=jax.ShapeDtypeStruct(blocks.shape, blocks.dtype),
        input_output_aliases={0: 0},
        name="settle",
    )(blocks)


def body(
    amplitudes,
    integrals,
    pair_orbitals,
    pair_of_triple,
    live_count,
    k_orbital,
    occ_irrep,
    occ_energy,
    vir_energy,
):
    irr_local = amplitudes.shape[1]
    irreps, width = vir_energy.shape
    slab = integrals.shape[4] // width
    per_dev = pair_of_triple.shape[0]
    trip, dens = lax.axis_size("trip"), lax.axis_size("dens")
    trip_bits = len(far_bits("trip"))
    triple_total = per_dev * trip
    sides = 2 if irr_local > 1 else 1
    share = irr_local // sides
    together = lax.optimization_barrier
    my_trip, my_dens = lax.axis_index("trip"), lax.axis_index("dens")

    own_meta = jnp.concatenate([pair_of_triple, live_count, k_orbital])
    meta = jnp.stack([own_meta, partner(own_meta, "trip", 1)])
    place = jnp.stack([my_trip, my_dens]).astype(jnp.int32)
    plan, ijk = make_plan(per_dev, dens, trip_bits, place, meta, pair_orbitals.reshape(-1), occ_irrep, occ_energy)

    vir_col = jnp.pad(vir_energy, ((0, 0), (0, block_rows(width) - width)))[:, :, None]
    vir_col = jnp.broadcast_to(vir_col, vir_col.shape[:2] + (LANES,))
    vir_mine = lax.dynamic_slice_in_dim(vir_energy, my_dens * irr_local, irr_local, 0)[:, :slab]
    y_table = jnp.repeat(vir_energy, slab, axis=1)[:, None, :] + jnp.tile(vir_mine, (1, width))[None, :, :]
    y_table = y_table.reshape(irreps * irr_local, 1, width * slab)

    amps = pack_blocks(amplitudes.reshape(irr_local, width, width))[None]
    moves = [("trip", bit) for bit in reversed(far_bits("trip"))] + [("dens", bit) for bit in all_bits("dens")]
    moves.append(("trip", 1))
    sent = own = recv = None
    for at, (axis, bit) in enumerate(moves):
        if at == 0 and sides > 1:
            amps, source = together((amps, integrals))
            got, sent = together((partner(amps, axis, bit), source[:, share:]))
            sent = partner(sent, "trip", 1)
        elif at == 1:
            amps, source = together((amps, integrals))
            got, own = together((partner(amps, axis, bit), settle(source)))
        elif at == len(moves) - 2 and sides > 1:
            amps, sent = together((amps, sent))
            got, recv = together((partner(amps, axis, bit), settle(sent)))
        else:
            got = partner(amps, axis, bit)
        amps = jnp.concatenate([amps, got])
    amps = amps.reshape((-1,) + amps.shape[2:])
    blocks = [own, recv][:sides]

    halvings = [("trip", 1)] + [("dens", bit) for bit in reversed(all_bits("dens"))]
    halvings += [("trip", bit) for bit in far_bits("trip")]
    running = []
    for stage in range(irr_local + len(halvings)):
        received = []
        for chunk, terms in enumerate(running):
            if stage - chunk <= len(halvings):
                axis, bit = halvings[stage - chunk - 1]
                received.append((chunk, partner(terms[terms.shape[0] // 2 :], axis, bit)))
        if stage < irr_local:
            dims = (width, per_dev, irr_local, dens, trip_bits, sides, stage)
            if running:
                held = together((place, *running))
                place, running = held[0], list(held[1:])
            new = pair_terms(dims, place, plan, ijk, amps, vir_col, y_table, blocks)
            held = together((new, *[got for _, got in received]))
            new = held[0]
            received = [(chunk, got) for (chunk, _), got in zip(received, held[1:])]
        for chunk, got in received:
            running[chunk] = running[chunk][: got.shape[0]] + got
        if stage < irr_local:
            running.append(new)
    terms = jnp.concatenate(running)

    orbitals = lax.dynamic_index_in_dim(pair_orbitals, my_trip, 0, keepdims=False)
    ij_irrep = jnp.bitwise_xor(occ_irrep[orbitals[0]], occ_irrep[orbitals[1]])
    local = jnp.arange(irr_local, dtype=jnp.int32)
    order = jnp.bitwise_xor(local, ij_irrep % irr_local)
    mine = jnp.take(unpack_blocks(terms, width), order, axis=0)
    amps_own = amps.reshape((2, dens, 1 << trip_bits, irr_local) + amps.shape[1:])[0, :, 0]
    amps_own = lax.dynamic_index_in_dim(amps_own, ij_irrep // irr_local, 0, keepdims=False)
    amps_own = jnp.take(unpack_blocks(amps_own, width), order, axis=0).astype(jnp.float32)
    density = jnp.einsum(
        "gad,gde->gae", mine, amps_own, precision=lax.Precision.HIGHEST, preferred_element_type=jnp.float32
    )
    density = density.reshape(irr_local, width * width)
    for bit in all_bits("trip"):
        density = density + partner(density, "trip", bit)
    return (mine.reshape(1, irr_local, width * width), density / triple_total)


def solution(mesh):
    in_specs = (
        P("trip", "dens", None),
        P("trip", "dens", None, None, None),
        P(),
        P("trip"),
        P("trip"),
        P("trip"),
        P(),
        P(),
        P(),
    )
    out_specs = (P("trip", "dens", None), P("dens", None))
    return jax.shard_map(body, mesh=mesh, in_specs=in_specs, out_specs=out_specs, check_vma=False)
```

```python
import jax
import jax.numpy as jnp
from jax import lax
from jax.experimental import pallas as pl
from jax.experimental.pallas import tpu as pltpu
from jax.sharding import PartitionSpec as P

LANES = 128
MAIN = 64


def round_up(value, step):
    return -(-value // step) * step


def block_rows(width):
    return round_up(width, 16)


def packed_rows(width):
    return block_rows(width) // 2 + 8


def pack_blocks(blocks):
    width = blocks.shape[-1]
    rows, rest = block_rows(width), width - MAIN
    lead = blocks.shape[:-2]
    pad = [(0, 0)] * len(lead)
    blocks = jnp.pad(blocks, pad + [(0, rows - width), (0, 0)])
    main = jnp.concatenate([blocks[..., : rows // 2, :MAIN], blocks[..., rows // 2 :, :MAIN]], axis=-1)
    tail = blocks[..., MAIN:].reshape(lead + (rows // 8, 8, rest))
    tail = jnp.swapaxes(tail, -3, -2).reshape(lead + (8, rows // 8 * rest))
    tail = jnp.pad(tail, pad + [(0, 0), (0, LANES - rows // 8 * rest)])
    return jnp.concatenate([main, tail], axis=-2)


def unpack_blocks(packed, width):
    rows, rest = block_rows(width), width - MAIN
    lead = packed.shape[:-2]
    main = jnp.concatenate([packed[..., : rows // 2, :MAIN], packed[..., : rows // 2, MAIN:]], axis=-2)
    tail = packed[..., rows // 2 :, : rows // 8 * rest].reshape(lead + (8, rows // 8, rest))
    tail = jnp.swapaxes(tail, -3, -2).reshape(lead + (rows, rest))
    return jnp.concatenate([main, tail], axis=-1)[..., :width, :]


def partner(value, axis, bit):
    count = lax.axis_size(axis)
    return lax.ppermute(value, axis, [(i, i ^ bit) for i in range(count)])


def far_bits(axis):
    bits, bit = [], 2
    while bit < lax.axis_size(axis):
        bits.append(bit)
        bit *= 2
    return bits


def all_bits(axis):
    return [1] + far_bits(axis) if lax.axis_size(axis) > 1 else []


def reversed_bits(value, count):
    out = jnp.int32(0)
    for b in range(count):
        out = out | (((value >> b) & 1) << (count - 1 - b))
    return out


def plan_kernel(
    per_dev, dens, trip_bits, place_ref, meta_ref, pairs_ref, irrep_ref, energy_ref, plan_ref, ijk_ref, list_ref
):
    mine = place_ref[0]
    plan_ref[4 + 8 * per_dev] = irrep_ref[pairs_ref[2 * mine]] ^ irrep_ref[pairs_ref[2 * mine + 1]]
    for who in range(2):
        k_orbital = meta_ref[who, per_dev + 1]
        live = meta_ref[who, per_dev]
        size = jnp.int32(0)
        for s in range(per_dev):
            pair = meta_ref[who, s]
            fresh = s < live
            for earlier in range(s):
                fresh = jnp.logical_and(fresh, meta_ref[who, earlier] != pair)

            @pl.when(fresh)
            def _():
                list_ref[size] = pair

            size = size + fresh.astype(jnp.int32)
        plan_ref[who] = size
        plan_ref[2 + who] = irrep_ref[k_orbital]
        for j in range(per_dev):
            at = 4 + 4 * (who * per_dev + j)

            @pl.when(j < size)
            def _():
                pair = list_ref[j]
                orb_i, orb_j = pairs_ref[2 * pair], pairs_ref[2 * pair + 1]
                gap = pair ^ place_ref[0]
                copies = jnp.int32(0)
                for s in range(per_dev):
                    same = jnp.logical_and(meta_ref[who, s] == pair, s < live)
                    copies = copies + same.astype(jnp.int32)
                plan_ref[at] = irrep_ref[orb_i] ^ irrep_ref[orb_j] ^ irrep_ref[k_orbital]
                plan_ref[at + 1] = (gap & 1) * dens
                plan_ref[at + 2] = reversed_bits(gap >> 1, trip_bits)
                plan_ref[at + 3] = copies
                ijk_ref[who * per_dev + j] = energy_ref[orb_i] + energy_ref[orb_j] + energy_ref[k_orbital]


def make_plan(per_dev, dens, trip_bits, place, meta, pairs, irreps, energies):
    smem = pl.BlockSpec(memory_space=pltpu.SMEM)
    return pl.pallas_call(
        lambda *refs: plan_kernel(per_dev, dens, trip_bits, *refs),
        in_specs=[smem] * 5,
        out_specs=[smem] * 2,
        out_shape=[
            jax.ShapeDtypeStruct((5 + 8 * per_dev,), jnp.int32),
            jax.ShapeDtypeStruct((2 * per_dev,), jnp.float32),
        ],
        scratch_shapes=[pltpu.SMEM((per_dev,), jnp.int32)],
        name="plan",
    )(place, meta, pairs, irreps, energies)


def unpacked_rows(packed, width):
    half, rest = block_rows(width) // 2, width - MAIN
    lane = lax.broadcasted_iota(jnp.int32, (8, LANES), 1)
    main, tail = packed[:half], packed[half:]
    turned = pltpu.roll(main, LANES - MAIN, 1)
    pieces = []
    for q in range(block_rows(width) // 8):
        left = main[8 * q : 8 * q + 8] if 8 * q < half else turned[8 * q - half : 8 * q - half + 8]
        right = pltpu.roll(tail, (MAIN - rest * q) % LANES, 1)
        pieces.append(jnp.where(lane < MAIN, left, right))
    return pieces


def finish_kernel(width, irr_local, trip_bits, plan_ref, amp_ref, *refs):
    terms_refs = refs[:irr_local]
    lambda_ref, density_ref, held, sem = refs[irr_local:]
    mix = plan_ref[plan_ref.shape[0] - 1]
    first = (mix // irr_local) * (irr_local << trip_bits)
    copy = pltpu.make_async_copy(amp_ref.at[pl.ds(first, irr_local)], held, sem)
    copy.start()
    copy.wait()
    for chunk in range(irr_local):
        local = chunk ^ (mix & (irr_local - 1))
        terms = jnp.concatenate(unpacked_rows(terms_refs[chunk][0], width), axis=0)[:width, :width]
        other = jnp.concatenate(unpacked_rows(held[chunk].astype(jnp.float32), width), axis=0)[:width, :width]
        other = other.astype(jnp.bfloat16)
        total = jnp.zeros((width, width), jnp.float32)
        left = terms
        for _ in range(3):
            piece = left.astype(jnp.bfloat16)
            left = left - piece.astype(jnp.float32)
            total = total + jnp.dot(piece, other, preferred_element_type=jnp.float32)
        lambda_ref[local] = terms
        density_ref[local] = total


def finish(width, trip_bits, plan, amps, parts):
    irr_local = len(parts)
    smem = pl.BlockSpec(memory_space=pltpu.SMEM)
    vmem = pl.BlockSpec(memory_space=pltpu.VMEM)
    return pl.pallas_call(
        lambda *refs: finish_kernel(width, irr_local, trip_bits, *refs),
        in_specs=[smem, pl.BlockSpec(memory_space=pl.ANY)] + [vmem] * irr_local,
        out_specs=[vmem] * 2,
        out_shape=[jax.ShapeDtypeStruct((irr_local, width, width), jnp.float32)] * 2,
        scratch_shapes=[
            pltpu.VMEM((irr_local,) + amps.shape[1:], amps.dtype),
            pltpu.SemaphoreType.DMA,
        ],
        compiler_params=pltpu.CompilerParams(vmem_limit_bytes=16 * 2**20),
        name="finish",
    )(plan, amps, *parts)


def term_kernel(
    dims,
    place_ref,
    plan_ref,
    ijk_ref,
    amp_ref,
    vir_ref,
    y_ref,
    *refs,
):
    width, per_dev, irr_local, dens, trip_bits, sides, chunk, whos = dims
    block_refs = refs[: len(whos)]
    base_ref = refs[len(whos)] if whos[0] > 0 else None
    out_ref, tile32, tile16, xcol, lam, gbuf, sems = refs[-7:]
    rows = block_rows(width)
    half, rest, groups = rows // 2, width - MAIN, rows // 8
    share, irreps = irr_local // sides, irr_local * dens
    low_mask = irr_local - 1
    steps = len(whos) * dens
    step = pl.program_id(0)
    my_dens = place_ref[1]

    def position(at):
        who, high = whos[0] + at // dens, at % dens
        return who, high * irr_local + (chunk ^ (plan_ref[2 + who] & low_mask))

    def arrive(slot, part):
        pltpu.make_async_copy(block_refs[0].at[0, 0, 0], gbuf.at[slot, part], sems.at[slot, part]).wait()

    def fetch(at):
        who, h = position(at)
        slot = at % 2
        for part in range(share):
            for side, ref in zip(whos, block_refs):
                b_irrep = h ^ (my_dens * irr_local + side * share + part)

                @pl.when(who == side)
                def _():
                    pltpu.make_async_copy(
                        ref.at[0, part, b_irrep], gbuf.at[slot, part], sems.at[slot, part]
                    ).start()

    @pl.when(step == 0)
    def _():
        fetch(step)
        out_ref[...] = jnp.zeros_like(out_ref) if base_ref is None else base_ref[...]

    @pl.when(step + 1 < steps)
    def _():
        fetch(step + 1)

    who, h = position(step)
    slot = step % 2
    size = plan_ref[who]
    lane = lax.broadcasted_iota(jnp.int32, (8, LANES), 1)
    wide = lax.broadcasted_iota(jnp.int32, (half, LANES), 1)

    def of_slot(j):
        at = 4 + 4 * (who * per_dev + j)
        a_irrep = h ^ plan_ref[at]
        spot = (plan_ref[at + 1] + ((a_irrep // irr_local) ^ my_dens)) * (1 << trip_bits) + plan_ref[at + 2]
        return a_irrep, spot, plan_ref[at + 3]

    for live in range(1, per_dev + 1):
        used = round_up(width * live, 16)

        @pl.when(size == live)
        def _():
            for j in range(live):
                a_irrep, spot, _ = of_slot(j)
                packed = amp_ref[spot * irr_local + (a_irrep & low_mask)].astype(jnp.float32)
                for q, piece in enumerate(unpacked_rows(packed, width)):
                    tile32[width * j + 8 * q : width * j + 8 * q + 8, :] = piece
                xcol[width * j : width * j + rows, :] = ijk_ref[who * per_dev + j] - vir_ref[a_irrep]
            tile16[:used, :] = tile32[:used, :width].astype(jnp.bfloat16)

            def one(part, carry):
                arrive(slot, part)
                c_local = who * share + part
                y_row = (h ^ (my_dens * irr_local + c_local)) * irr_local + c_local
                left = tile16[:used, :]
                acc = jnp.zeros((used, width), jnp.float32)
                total = gbuf.shape[3]
                for start in range(0, total, 256):
                    stop = min(start + 256, total)
                    g = gbuf[slot, part, :, start:stop]
                    w = jnp.dot(left, g, preferred_element_type=jnp.float32)
                    x = xcol[:used, :]
                    x = jnp.concatenate([x, x], axis=1)[:, : stop - start]
                    z = (w / (x - y_ref[y_row][:, start:stop])).astype(jnp.bfloat16)
                    acc = acc + lax.dot_general(
                        z, g, (((1,), (1,)), ((), ())), preferred_element_type=jnp.float32
                    )

                @pl.when(part == 0)
                def _():
                    lam[:used, :width] = acc

                @pl.when(part > 0)
                def _():
                    lam[:used, :width] = lam[:used, :width] + acc

                return carry

            lax.fori_loop(0, share, one, 0)

            for j in range(live):
                _, spot, copies = of_slot(j)
                weight = copies.astype(jnp.float32)
                tail = jnp.zeros((8, LANES), jnp.float32)
                for q in range(groups):
                    block = lam[width * j + 8 * q : width * j + 8 * q + 8, :]
                    moved = pltpu.roll(block, (rest * q - MAIN) % LANES, 1)
                    here = jnp.logical_and(lane >= rest * q, lane < rest * q + rest)
                    tail = jnp.where(here, moved, tail)
                top = lam[width * j : width * j + half, :]
                low = pltpu.roll(lam[width * j + half : width * j + rows, :], MAIN, 1)
                main = jnp.where(wide < MAIN, top, low)
                out_ref[spot, :half, :] = out_ref[spot, :half, :] + weight * main
                out_ref[spot, half:, :] = out_ref[spot, half:, :] + weight * tail


def pair_terms(dims, place, plan, ijk, amps, vir_col, y_table, blocks, base):
    width, per_dev, irr_local, dens, trip_bits, sides, _, whos = dims
    blocks = [blocks[who] for who in whos]
    bases = [base] if whos[0] > 0 else []
    share = irr_local // sides
    tall = round_up(width * per_dev + block_rows(width) - width, 16)
    spots = 2 * dens * (1 << trip_bits)
    smem = pl.BlockSpec(memory_space=pltpu.SMEM)
    vmem = pl.BlockSpec(memory_space=pltpu.VMEM)
    hbm = pl.BlockSpec(memory_space=pltpu.HBM)
    return pl.pallas_call(
        lambda *refs: term_kernel(dims, *refs),
        grid=(len(whos) * dens,),
        in_specs=[smem] * 3 + [vmem] * 3 + [hbm] * len(blocks) + [vmem] * len(bases),
        out_specs=vmem,
        out_shape=jax.ShapeDtypeStruct((spots, packed_rows(width), LANES), jnp.float32),
        scratch_shapes=[
            pltpu.VMEM((tall, LANES), jnp.float32),
            pltpu.VMEM((tall, width), jnp.bfloat16),
            pltpu.VMEM((tall, LANES), jnp.float32),
            pltpu.VMEM((tall, LANES), jnp.float32),
            pltpu.VMEM((2, share) + blocks[0].shape[3:], jnp.bfloat16),
            pltpu.SemaphoreType.DMA((2, share)),
        ],
        compiler_params=pltpu.CompilerParams(vmem_limit_bytes=48 * 2**20),
        cost_estimate=pl.CostEstimate(flops=7 * 10**9 * len(whos), bytes_accessed=10**7, transcendentals=0),
        name="pair_terms",
    )(place, plan, ijk, amps, vir_col, y_table, *blocks, *bases)


def settle(blocks):
    hbm = pl.BlockSpec(memory_space=pltpu.HBM)
    return pl.pallas_call(
        lambda source, target: None,
        in_specs=[hbm],
        out_specs=hbm,
        out_shape=jax.ShapeDtypeStruct(blocks.shape, blocks.dtype),
        input_output_aliases={0: 0},
        name="settle",
    )(blocks)


def body(
    amplitudes,
    integrals,
    pair_orbitals,
    pair_of_triple,
    live_count,
    k_orbital,
    occ_irrep,
    occ_energy,
    vir_energy,
):
    irr_local = amplitudes.shape[1]
    irreps, width = vir_energy.shape
    slab = integrals.shape[4] // width
    per_dev = pair_of_triple.shape[0]
    trip, dens = lax.axis_size("trip"), lax.axis_size("dens")
    trip_bits = len(far_bits("trip"))
    triple_total = per_dev * trip
    sides = 2 if irr_local > 1 else 1
    share = irr_local // sides
    together = lax.optimization_barrier
    my_trip, my_dens = lax.axis_index("trip"), lax.axis_index("dens")

    own_meta = jnp.concatenate([pair_of_triple, live_count, k_orbital])
    meta = jnp.stack([own_meta, partner(own_meta, "trip", 1)])
    place = jnp.stack([my_trip, my_dens]).astype(jnp.int32)
    plan, ijk = make_plan(per_dev, dens, trip_bits, place, meta, pair_orbitals.reshape(-1), occ_irrep, occ_energy)

    vir_col = jnp.pad(vir_energy, ((0, 0), (0, block_rows(width) - width)))[:, :, None]
    vir_col = jnp.broadcast_to(vir_col, vir_col.shape[:2] + (LANES,))
    vir_mine = lax.dynamic_slice_in_dim(vir_energy, my_dens * irr_local, irr_local, 0)[:, :slab]
    column = jnp.arange(width * slab, dtype=jnp.int32)[None, :]
    chosen = [
        column // slab == jnp.arange(width, dtype=jnp.int32)[:, None],
        column % slab == jnp.arange(slab, dtype=jnp.int32)[:, None],
    ]
    energies = [
        jnp.broadcast_to(vir_energy[:, None, :], (irreps, irr_local, width)),
        jnp.broadcast_to(vir_mine[None, :, :], (irreps, irr_local, slab)),
    ]
    y_table = jnp.dot(
        jnp.concatenate(energies, axis=2).reshape(irreps * irr_local, width + slab),
        jnp.concatenate(chosen, axis=0).astype(jnp.float32),
        precision=lax.Precision.HIGHEST,
    ).reshape(irreps * irr_local, 1, width * slab)

    amps = pack_blocks(amplitudes.reshape(irr_local, width, width))[None]
    moves = [("trip", bit) for bit in reversed(far_bits("trip"))] + [("dens", bit) for bit in all_bits("dens")]
    moves.append(("trip", 1))
    sent = own = recv = None
    for at, (axis, bit) in enumerate(moves):
        if at == 0 and sides > 1:
            amps, source = together((amps, integrals))
            got, sent = together((partner(amps, axis, bit), source[:, share:]))
            sent = partner(sent, "trip", 1)
        elif at == 1:
            amps, source = together((amps, integrals))
            got, own = together((partner(amps, axis, bit), settle(source)))
        elif at == len(moves) - 2 and sides > 1:
            amps, sent = together((amps, sent))
            got, recv = together((partner(amps, axis, bit), settle(sent)))
        elif at == 2:
            got = partner(amps, axis, bit)
            got, plan, ijk, y_table, vir_col = together((got, plan, ijk, y_table, vir_col))
        else:
            got = partner(amps, axis, bit)
        amps = jnp.concatenate([amps, got])
    amps = amps.reshape((-1,) + amps.shape[2:])
    blocks = [own, recv][:sides]

    halvings = [("trip", 1)] + [("dens", bit) for bit in reversed(all_bits("dens"))]
    halvings += [("trip", bit) for bit in far_bits("trip")]
    both = tuple(range(sides))
    calls = []
    for chunk in range(irr_local):
        calls += [(chunk, both)] if chunk < irr_local - 1 else [(chunk, (who,)) for who in both]

    def halve(entry, got):
        return (entry[0][: got.shape[0]] + got, entry[1] + 1)

    def upper(entry):
        axis, bit = halvings[entry[1]]
        return partner(entry[0][entry[0].shape[0] // 2 :], axis, bit)

    running, base = [], None
    for chunk, whos in calls:
        active = [i for i, entry in enumerate(running) if entry[1] < len(halvings)]
        if active:
            held = together((place, *[running[i][0] for i in active]))
            place = held[0]
            for i, terms in zip(active, held[1:]):
                running[i] = (terms, running[i][1])
        received = [upper(running[i]) for i in active]
        dims = (width, per_dev, irr_local, dens, trip_bits, sides, chunk, whos)
        held = together((pair_terms(dims, place, plan, ijk, amps, vir_col, y_table, blocks, base), *received))
        base = held[0]
        for i, got in zip(active, held[1:]):
            running[i] = halve(running[i], got)
        if whos[-1] == sides - 1:
            running.append((base, 0))
    for _ in halvings:
        for i, entry in enumerate(running):
            if entry[1] < len(halvings):
                running[i] = halve(entry, upper(entry))
    mine, density = finish(width, trip_bits, plan, amps, [entry[0] for entry in running])
    density = density.reshape(irr_local, width * width)
    for bit in all_bits("trip"):
        density = density + partner(density, "trip", bit)
    return (mine.reshape(1, irr_local, width * width), density / triple_total)


def solution(mesh):
    in_specs = (
        P("trip", "dens", None),
        P("trip", "dens", None, None, None),
        P(),
        P("trip"),
        P("trip"),
        P("trip"),
        P(),
        P(),
        P(),
    )
    out_specs = (P("trip", "dens", None), P("dens", None))
    return jax.shard_map(body, mesh=mesh, in_specs=in_specs, out_specs=out_specs, check_vma=False)
```

```python
import jax
import jax.numpy as jnp
from jax import lax
from jax.experimental import pallas as pl
from jax.experimental.pallas import tpu as pltpu
from jax.sharding import PartitionSpec as P

LANES = 128
MAIN = 64


def round_up(value, step):
    return -(-value // step) * step


def block_rows(width):
    return round_up(width, 16)


def packed_rows(width):
    return block_rows(width) // 2 + 8


def pack_blocks(blocks):
    width = blocks.shape[-1]
    rows, rest = block_rows(width), width - MAIN
    lead = blocks.shape[:-2]
    pad = [(0, 0)] * len(lead)
    blocks = jnp.pad(blocks, pad + [(0, rows - width), (0, 0)])
    main = jnp.concatenate([blocks[..., : rows // 2, :MAIN], blocks[..., rows // 2 :, :MAIN]], axis=-1)
    tail = blocks[..., MAIN:].reshape(lead + (rows // 8, 8, rest))
    tail = jnp.swapaxes(tail, -3, -2).reshape(lead + (8, rows // 8 * rest))
    tail = jnp.pad(tail, pad + [(0, 0), (0, LANES - rows // 8 * rest)])
    return jnp.concatenate([main, tail], axis=-2)


def unpack_blocks(packed, width):
    rows, rest = block_rows(width), width - MAIN
    lead = packed.shape[:-2]
    main = jnp.concatenate([packed[..., : rows // 2, :MAIN], packed[..., : rows // 2, MAIN:]], axis=-2)
    tail = packed[..., rows // 2 :, : rows // 8 * rest].reshape(lead + (8, rows // 8, rest))
    tail = jnp.swapaxes(tail, -3, -2).reshape(lead + (rows, rest))
    return jnp.concatenate([main, tail], axis=-1)[..., :width, :]


def partner(value, axis, bit):
    count = lax.axis_size(axis)
    return lax.ppermute(value, axis, [(i, i ^ bit) for i in range(count)])


def far_bits(axis):
    bits, bit = [], 2
    while bit < lax.axis_size(axis):
        bits.append(bit)
        bit *= 2
    return bits


def all_bits(axis):
    return [1] + far_bits(axis) if lax.axis_size(axis) > 1 else []


def reversed_bits(value, count):
    out = jnp.int32(0)
    for b in range(count):
        out = out | (((value >> b) & 1) << (count - 1 - b))
    return out


def plan_kernel(
    per_dev, dens, trip_bits, place_ref, meta_ref, pairs_ref, irrep_ref, energy_ref, plan_ref, ijk_ref, list_ref
):
    for r in range(1 << trip_bits):
        pair = place_ref[0] ^ (int(f"{r:0{trip_bits}b}"[::-1], 2) << 1)
        plan_ref[4 + 8 * per_dev + r] = irrep_ref[pairs_ref[2 * pair]] ^ irrep_ref[pairs_ref[2 * pair + 1]]
    for who in range(2):
        k_orbital = meta_ref[who, per_dev + 1]
        live = meta_ref[who, per_dev]
        size = jnp.int32(0)
        for s in range(per_dev):
            pair = meta_ref[who, s]
            fresh = s < live
            for earlier in range(s):
                fresh = jnp.logical_and(fresh, meta_ref[who, earlier] != pair)

            @pl.when(fresh)
            def _():
                list_ref[size] = pair

            size = size + fresh.astype(jnp.int32)
        plan_ref[who] = size
        plan_ref[2 + who] = irrep_ref[k_orbital]
        for j in range(per_dev):
            at = 4 + 4 * (who * per_dev + j)

            @pl.when(j < size)
            def _():
                pair = list_ref[j]
                orb_i, orb_j = pairs_ref[2 * pair], pairs_ref[2 * pair + 1]
                gap = pair ^ place_ref[0]
                copies = jnp.int32(0)
                for s in range(per_dev):
                    same = jnp.logical_and(meta_ref[who, s] == pair, s < live)
                    copies = copies + same.astype(jnp.int32)
                plan_ref[at] = irrep_ref[orb_i] ^ irrep_ref[orb_j] ^ irrep_ref[k_orbital]
                plan_ref[at + 1] = (gap & 1) * dens
                plan_ref[at + 2] = reversed_bits(gap >> 1, trip_bits)
                plan_ref[at + 3] = copies
                ijk_ref[who * per_dev + j] = energy_ref[orb_i] + energy_ref[orb_j] + energy_ref[k_orbital]


def make_plan(per_dev, dens, trip_bits, place, meta, pairs, irreps, energies):
    smem = pl.BlockSpec(memory_space=pltpu.SMEM)
    return pl.pallas_call(
        lambda *refs: plan_kernel(per_dev, dens, trip_bits, *refs),
        in_specs=[smem] * 5,
        out_specs=[smem] * 2,
        out_shape=[
            jax.ShapeDtypeStruct((4 + 8 * per_dev + (1 << trip_bits),), jnp.int32),
            jax.ShapeDtypeStruct((2 * per_dev,), jnp.float32),
        ],
        scratch_shapes=[pltpu.SMEM((per_dev,), jnp.int32)],
        name="plan",
    )(place, meta, pairs, irreps, energies)


def unpacked_rows(packed, width):
    half, rest = block_rows(width) // 2, width - MAIN
    lane = lax.broadcasted_iota(jnp.int32, (8, LANES), 1)
    main, tail = packed[:half], packed[half:]
    turned = pltpu.roll(main, LANES - MAIN, 1)
    pieces = []
    for q in range(block_rows(width) // 8):
        left = main[8 * q : 8 * q + 8] if 8 * q < half else turned[8 * q - half : 8 * q - half + 8]
        right = pltpu.roll(tail, (MAIN - rest * q) % LANES, 1)
        pieces.append(jnp.where(lane < MAIN, left, right))
    return pieces


def density_kernel(width, trip_bits, irr_local, chunks, plan_ref, amp_ref, *refs):
    terms_refs, density_ref = refs[: len(chunks)], refs[-1]
    density_ref[...] = refs[len(chunks)][...] if len(refs) > len(chunks) + 1 else jnp.zeros_like(density_ref)
    spots = 1 << trip_bits
    for r in range(spots):
        mix = plan_ref[plan_ref.shape[0] - spots + r]
        for chunk, terms_ref in zip(chunks, terms_refs):
            packed = amp_ref[((mix // irr_local) * spots + r) * irr_local + chunk].astype(jnp.float32)
            other = jnp.concatenate(unpacked_rows(packed, width), axis=0)[:width, :width].astype(jnp.bfloat16)
            left = jnp.concatenate(unpacked_rows(terms_ref[r], width), axis=0)[:width, :width]
            total = jnp.zeros((width, width), jnp.float32)
            for _ in range(3):
                piece = left.astype(jnp.bfloat16)
                left = left - piece.astype(jnp.float32)
                total = total + jnp.dot(piece, other, preferred_element_type=jnp.float32)
            local = chunk ^ (mix & (irr_local - 1))
            density_ref[local] = density_ref[local] + total


def density_terms(width, trip_bits, irr_local, chunks, plan, amps, parts, base):
    smem = pl.BlockSpec(memory_space=pltpu.SMEM)
    vmem = pl.BlockSpec(memory_space=pltpu.VMEM)
    bases = [] if base is None else [base]
    near = pl.BlockSpec((amps.shape[0] // 2,) + amps.shape[1:], lambda i: (0, 0, 0))
    return pl.pallas_call(
        lambda *refs: density_kernel(width, trip_bits, irr_local, chunks, *refs),
        grid=(1,),
        in_specs=[smem, near] + [vmem] * (len(parts) + len(bases)),
        out_specs=vmem,
        out_shape=jax.ShapeDtypeStruct((irr_local, width, width), jnp.float32),
        compiler_params=pltpu.CompilerParams(vmem_limit_bytes=24 * 2**20),
        name="density_terms",
    )(plan, amps, *parts, *bases)


def finish_kernel(width, trip_bits, plan_ref, *refs):
    irr_local = len(refs) - 1
    mix = plan_ref[plan_ref.shape[0] - (1 << trip_bits)]
    for chunk in range(irr_local):
        rows = jnp.concatenate(unpacked_rows(refs[chunk][0], width), axis=0)
        refs[-1][chunk ^ (mix & (irr_local - 1))] = rows[:width, :width]


def finish(width, trip_bits, plan, parts):
    vmem = pl.BlockSpec(memory_space=pltpu.VMEM)
    return pl.pallas_call(
        lambda *refs: finish_kernel(width, trip_bits, *refs),
        in_specs=[pl.BlockSpec(memory_space=pltpu.SMEM)] + [vmem] * len(parts),
        out_specs=vmem,
        out_shape=jax.ShapeDtypeStruct((len(parts), width, width), jnp.float32),
        name="finish",
    )(plan, *parts)


def term_kernel(
    dims,
    place_ref,
    plan_ref,
    ijk_ref,
    amp_ref,
    vir_ref,
    y_ref,
    *refs,
):
    width, per_dev, irr_local, dens, trip_bits, sides, chunk, whos = dims
    block_refs = refs[: len(whos)]
    base_ref = refs[len(whos)] if whos[0] > 0 else None
    out_ref, tile32, tile16, xcol, lam, gbuf, sems = refs[-7:]
    rows = block_rows(width)
    half, rest, groups = rows // 2, width - MAIN, rows // 8
    share, irreps = irr_local // sides, irr_local * dens
    low_mask = irr_local - 1
    steps = len(whos) * dens
    step = pl.program_id(0)
    my_dens = place_ref[1]

    def position(at):
        who, high = whos[0] + at // dens, at % dens
        return who, high * irr_local + (chunk ^ (plan_ref[2 + who] & low_mask))

    def arrive(slot, part):
        pltpu.make_async_copy(block_refs[0].at[0, 0, 0], gbuf.at[slot, part], sems.at[slot, part]).wait()

    def fetch(at):
        who, h = position(at)
        slot = at % 2
        for part in range(share):
            for side, ref in zip(whos, block_refs):
                b_irrep = h ^ (my_dens * irr_local + side * share + part)

                @pl.when(who == side)
                def _():
                    pltpu.make_async_copy(
                        ref.at[0, part, b_irrep], gbuf.at[slot, part], sems.at[slot, part]
                    ).start()

    @pl.when(step == 0)
    def _():
        fetch(step)
        out_ref[...] = jnp.zeros_like(out_ref) if base_ref is None else base_ref[...]

    @pl.when(step + 1 < steps)
    def _():
        fetch(step + 1)

    who, h = position(step)
    slot = step % 2
    size = plan_ref[who]
    lane = lax.broadcasted_iota(jnp.int32, (8, LANES), 1)
    wide = lax.broadcasted_iota(jnp.int32, (half, LANES), 1)

    def of_slot(j):
        at = 4 + 4 * (who * per_dev + j)
        a_irrep = h ^ plan_ref[at]
        spot = (plan_ref[at + 1] + ((a_irrep // irr_local) ^ my_dens)) * (1 << trip_bits) + plan_ref[at + 2]
        return a_irrep, spot, plan_ref[at + 3]

    for live in range(1, per_dev + 1):
        used = round_up(width * live, 16)

        @pl.when(size == live)
        def _():
            for j in range(live):
                a_irrep, spot, _ = of_slot(j)
                packed = amp_ref[spot * irr_local + (a_irrep & low_mask)].astype(jnp.float32)
                for q, piece in enumerate(unpacked_rows(packed, width)):
                    tile32[width * j + 8 * q : width * j + 8 * q + 8, :] = piece
                xcol[width * j : width * j + rows, :] = ijk_ref[who * per_dev + j] - vir_ref[a_irrep]
            tile16[:used, :] = tile32[:used, :width].astype(jnp.bfloat16)

            def one(part, carry):
                arrive(slot, part)
                c_local = who * share + part
                y_row = (h ^ (my_dens * irr_local + c_local)) * irr_local + c_local
                left = tile16[:used, :]
                acc = jnp.zeros((used, width), jnp.float32)
                total = gbuf.shape[3]
                for start in range(0, total, 256):
                    stop = min(start + 256, total)
                    g = gbuf[slot, part, :, start:stop]
                    w = jnp.dot(left, g, preferred_element_type=jnp.float32)
                    x = xcol[:used, :]
                    x = jnp.concatenate([x, x], axis=1)[:, : stop - start]
                    z = (w / (x - y_ref[y_row][:, start:stop])).astype(jnp.bfloat16)
                    acc = acc + lax.dot_general(
                        z, g, (((1,), (1,)), ((), ())), preferred_element_type=jnp.float32
                    )

                @pl.when(part == 0)
                def _():
                    lam[:used, :width] = acc

                @pl.when(part > 0)
                def _():
                    lam[:used, :width] = lam[:used, :width] + acc

                return carry

            lax.fori_loop(0, share, one, 0)

            for j in range(live):
                _, spot, copies = of_slot(j)
                weight = copies.astype(jnp.float32)
                tail = jnp.zeros((8, LANES), jnp.float32)
                for q in range(groups):
                    block = lam[width * j + 8 * q : width * j + 8 * q + 8, :]
                    moved = pltpu.roll(block, (rest * q - MAIN) % LANES, 1)
                    here = jnp.logical_and(lane >= rest * q, lane < rest * q + rest)
                    tail = jnp.where(here, moved, tail)
                top = lam[width * j : width * j + half, :]
                low = pltpu.roll(lam[width * j + half : width * j + rows, :], MAIN, 1)
                main = jnp.where(wide < MAIN, top, low)
                out_ref[spot, :half, :] = out_ref[spot, :half, :] + weight * main
                out_ref[spot, half:, :] = out_ref[spot, half:, :] + weight * tail


def pair_terms(dims, place, plan, ijk, amps, vir_col, y_table, blocks, base):
    width, per_dev, irr_local, dens, trip_bits, sides, _, whos = dims
    blocks = [blocks[who] for who in whos]
    bases = [base] if whos[0] > 0 else []
    share = irr_local // sides
    tall = round_up(width * per_dev + block_rows(width) - width, 16)
    spots = 2 * dens * (1 << trip_bits)
    smem = pl.BlockSpec(memory_space=pltpu.SMEM)
    vmem = pl.BlockSpec(memory_space=pltpu.VMEM)
    hbm = pl.BlockSpec(memory_space=pltpu.HBM)
    return pl.pallas_call(
        lambda *refs: term_kernel(dims, *refs),
        grid=(len(whos) * dens,),
        in_specs=[smem] * 3 + [vmem] * 3 + [hbm] * len(blocks) + [vmem] * len(bases),
        out_specs=vmem,
        out_shape=jax.ShapeDtypeStruct((spots, packed_rows(width), LANES), jnp.float32),
        scratch_shapes=[
            pltpu.VMEM((tall, LANES), jnp.float32),
            pltpu.VMEM((tall, width), jnp.bfloat16),
            pltpu.VMEM((tall, LANES), jnp.float32),
            pltpu.VMEM((tall, LANES), jnp.float32),
            pltpu.VMEM((2, share) + blocks[0].shape[3:], jnp.bfloat16),
            pltpu.SemaphoreType.DMA((2, share)),
        ],
        compiler_params=pltpu.CompilerParams(vmem_limit_bytes=48 * 2**20),
        cost_estimate=pl.CostEstimate(flops=7 * 10**9 * len(whos), bytes_accessed=10**7, transcendentals=0),
        name="pair_terms",
    )(place, plan, ijk, amps, vir_col, y_table, *blocks, *bases)


def settle(blocks):
    hbm = pl.BlockSpec(memory_space=pltpu.HBM)
    return pl.pallas_call(
        lambda source, target: None,
        in_specs=[hbm],
        out_specs=hbm,
        out_shape=jax.ShapeDtypeStruct(blocks.shape, blocks.dtype),
        input_output_aliases={0: 0},
        name="settle",
    )(blocks)


def body(
    amplitudes,
    integrals,
    pair_orbitals,
    pair_of_triple,
    live_count,
    k_orbital,
    occ_irrep,
    occ_energy,
    vir_energy,
):
    irr_local = amplitudes.shape[1]
    irreps, width = vir_energy.shape
    slab = integrals.shape[4] // width
    per_dev = pair_of_triple.shape[0]
    trip, dens = lax.axis_size("trip"), lax.axis_size("dens")
    trip_bits = len(far_bits("trip"))
    triple_total = per_dev * trip
    sides = 2 if irr_local > 1 else 1
    share = irr_local // sides
    together = lax.optimization_barrier
    my_trip, my_dens = lax.axis_index("trip"), lax.axis_index("dens")

    own_meta = jnp.concatenate([pair_of_triple, live_count, k_orbital])
    meta = jnp.stack([own_meta, partner(own_meta, "trip", 1)])
    place = jnp.stack([my_trip, my_dens]).astype(jnp.int32)
    plan, ijk = make_plan(per_dev, dens, trip_bits, place, meta, pair_orbitals.reshape(-1), occ_irrep, occ_energy)

    vir_col = jnp.pad(vir_energy, ((0, 0), (0, block_rows(width) - width)))[:, :, None]
    vir_col = jnp.broadcast_to(vir_col, vir_col.shape[:2] + (LANES,))
    vir_mine = lax.dynamic_slice_in_dim(vir_energy, my_dens * irr_local, irr_local, 0)[:, :slab]
    column = jnp.arange(width * slab, dtype=jnp.int32)[None, :]
    chosen = [
        column // slab == jnp.arange(width, dtype=jnp.int32)[:, None],
        column % slab == jnp.arange(slab, dtype=jnp.int32)[:, None],
    ]
    energies = [
        jnp.broadcast_to(vir_energy[:, None, :], (irreps, irr_local, width)),
        jnp.broadcast_to(vir_mine[None, :, :], (irreps, irr_local, slab)),
    ]
    y_table = jnp.dot(
        jnp.concatenate(energies, axis=2).reshape(irreps * irr_local, width + slab),
        jnp.concatenate(chosen, axis=0).astype(jnp.float32),
        precision=lax.Precision.HIGHEST,
    ).reshape(irreps * irr_local, 1, width * slab)

    amps = pack_blocks(amplitudes.reshape(irr_local, width, width))[None]
    moves = [("trip", bit) for bit in reversed(far_bits("trip"))] + [("dens", bit) for bit in all_bits("dens")]
    moves.append(("trip", 1))
    sent = own = recv = None
    for at, (axis, bit) in enumerate(moves):
        if at == 0 and sides > 1:
            amps, source = together((amps, integrals))
            got, sent = together((partner(amps, axis, bit), source[:, share:]))
            sent = partner(sent, "trip", 1)
        elif at == 1:
            amps, source = together((amps, integrals))
            got, own = together((partner(amps, axis, bit), settle(source)))
        elif at == len(moves) - 2 and sides > 1:
            amps, sent = together((amps, sent))
            got, recv = together((partner(amps, axis, bit), settle(sent)))
        elif at == 2:
            got = partner(amps, axis, bit)
            got, plan, ijk, y_table, vir_col = together((got, plan, ijk, y_table, vir_col))
        else:
            got = partner(amps, axis, bit)
        amps = jnp.concatenate([amps, got])
    amps = amps.reshape((-1,) + amps.shape[2:])
    blocks = [own, recv][:sides]

    halvings = [("trip", 1)] + [("dens", bit) for bit in reversed(all_bits("dens"))]
    halvings += [("trip", bit) for bit in far_bits("trip")]
    both = tuple(range(sides))
    calls = []
    for chunk in range(irr_local):
        calls += [(chunk, both)] if chunk < irr_local - 1 else [(chunk, (who,)) for who in both]

    def halve(entry, got):
        return (entry[0][: got.shape[0]] + got, entry[1] + 1)

    def upper(entry):
        axis, bit = halvings[entry[1]]
        return partner(entry[0][entry[0].shape[0] // 2 :], axis, bit)

    running, base = [], None
    tapped = [None] * irr_local
    taps = 1 + len(all_bits("dens"))
    for chunk, whos in calls:
        active = [i for i, entry in enumerate(running) if entry[1] < len(halvings)]
        if active:
            held = together((place, *[running[i][0] for i in active]))
            place = held[0]
            for i, terms in zip(active, held[1:]):
                running[i] = (terms, running[i][1])
        received = [upper(running[i]) for i in active]
        dims = (width, per_dev, irr_local, dens, trip_bits, sides, chunk, whos)
        held = together((pair_terms(dims, place, plan, ijk, amps, vir_col, y_table, blocks, base), *received))
        base = held[0]
        for i, got in zip(active, held[1:]):
            running[i] = halve(running[i], got)
            if running[i][1] == taps:
                tapped[i] = running[i][0]
        if whos[-1] == sides - 1:
            running.append((base, 0))
    for _ in range(len(halvings) + 1):
        for i, entry in enumerate(running):
            if entry[1] == taps:
                tapped[i] = entry[0]
            if entry[1] < len(halvings):
                running[i] = halve(entry, upper(entry))
    early = tuple(range(irr_local - 1))
    density = None
    if early:
        density = density_terms(width, trip_bits, irr_local, early, plan, amps, tapped[:-1], None)
    density = density_terms(width, trip_bits, irr_local, (irr_local - 1,), plan, amps, tapped[-1:], density)
    density = density.reshape(irr_local, width * width)
    for bit in all_bits("trip"):
        density = density + partner(density, "trip", bit)
    mine = finish(width, trip_bits, plan, [entry[0] for entry in running])
    return (mine.reshape(1, irr_local, width * width), density / triple_total)


def solution(mesh):
    in_specs = (
        P("trip", "dens", None),
        P("trip", "dens", None, None, None),
        P(),
        P("trip"),
        P("trip"),
        P("trip"),
        P(),
        P(),
        P(),
    )
    out_specs = (P("trip", "dens", None), P("dens", None))
    return jax.shard_map(body, mesh=mesh, in_specs=in_specs, out_specs=out_specs, check_vma=False)
```
